256 devices in a mesh: row: 8 (over x, z_lo), col: 32 (over z_hi, y, core).
Axes of the slice: x: 4, y: 4, z: 8 (z_hi: 4, z_lo: 2; z = z_hi * 2 + z_lo), core: 2. Of those that a mesh axis runs over, the one named last changes fastest.
Arguments:
- tokens: bfloat16 [512, 12288], P('col', 'row'), may hold values from -6 to 6
- out_grad: bfloat16 [512, 12288], P('col', 'row'), may hold values from -6 to 6
- gate_w: bfloat16 [12288, 28672], P('row', 'col'), may hold values from -0.0546875 to 0.0546875
- up_w: bfloat16 [12288, 28672], P('row', 'col'), may hold values from -0.0546875 to 0.0546875
- down_w: bfloat16 [28672, 12288], P('col', 'row'), may hold values from -0.03125 to 0.03125
- gate_a: float32 [12288, 128], P(('row', 'col')), may hold values from -0.0546875 to 0.0546875
- up_a: float32 [12288, 128], P(('row', 'col')), may hold values from -0.0546875 to 0.0546875
- down_b_t: float32 [12288, 128], P(('row', 'col')), may hold values from -0.25 to 0.25
- gate_b: float32 [128, 28672], P('row', 'col'), may hold values from -0.25 to 0.25
- up_b: float32 [128, 28672], P('row', 'col'), may hold values from -0.25 to 0.25
- down_a_t: float32 [128, 28672], P('row', 'col'), may hold values from -0.03125 to 0.03125
Outputs:
- grad_tokens: float32 [512, 12288], P('col', 'row')
- grad_gate_a: float32 [12288, 128], P(('row', 'col'))
- grad_up_a: float32 [12288, 128], P(('row', 'col'))
- grad_gate_b: float32 [128, 28672], P('row', 'col')
- grad_up_b: float32 [128, 28672], P('row', 'col')
- grad_down_a_t: float32 [128, 28672], P('row', 'col')
- grad_down_b_t: float32 [12288, 128], P(('row', 'col'))
The draws below stay inside these ranges and needn't reach their ends.
All inputs are finite; a program needn't handle non-finite values.
Results may differ from the reference program's by a relative error of at most 0.0029.
Values may be sent and summed in bfloat16 or wider, within the bound.
No kernel may reach another device: no remote copies, remote signals or barrier semaphores. Data moves between devices by JAX's collectives and lax.ppermute only.
A program may use at most 128 MiB of HBM per device.

```python
import jax
import jax.numpy as jnp
from jax import lax

D = 12288
FF = 28672
R = 128
TOKENS = 512


def block_scale(stream_key, extent, pieces, smallest, top_value):
    gain = 1.0
    for dim, shards_of in pieces:
        steps = jax.random.uniform(jax.random.fold_in(jax.random.fold_in(stream_key, 6), dim), (shards_of,), jnp.float32, smallest / len(pieces), top_value / len(pieces))
        gain = gain * jnp.repeat(jnp.exp(steps), extent[dim] // shards_of).reshape((-1,) + (1,) * (len(extent) - 1 - dim))
    return gain


def scatter_about(key, extent, scale, limit, pieces=(), kind=jnp.bfloat16):
    array = jax.random.normal(key, extent, jnp.float32) * scale
    if len(pieces) > 0:
        array = block_scale(key, extent, pieces, -0.22, 0.18) * array
    return jnp.clip(array, min=-limit, max=limit).astype(kind)


def setup_inputs(seed: int = 0) -> dict:
    arg_keys = jax.random.split(jax.random.key(seed), 12)
    tokens = scatter_about(arg_keys[0], (TOKENS, D), 1.0, 6.0, ((0, 32), (1, 8)))
    out_grad = scatter_about(arg_keys[1], (TOKENS, D), 1.0, 6.0, ((0, 32), (1, 8)))
    gate_w = scatter_about(arg_keys[2], (D, FF), D ** -0.5, 0.0546875, ((0, 8), (1, 32)))
    up_w = scatter_about(arg_keys[3], (D, FF), D ** -0.5, 0.0546875, ((0, 8), (1, 32)))
    down_w = scatter_about(arg_keys[4], (FF, D), FF ** -0.5, 0.03125, ((0, 32), (1, 8)))
    gate_a = scatter_about(arg_keys[5], (D, R), D ** -0.5, 0.0546875, ((0, 256),), jnp.float32)
    up_a = scatter_about(arg_keys[6], (D, R), D ** -0.5, 0.0546875, ((0, 256),), jnp.float32)
    down_b_t = scatter_about(arg_keys[7], (D, R), (4 * R) ** -0.5, 0.25, ((0, 256),), jnp.float32)
    gate_b = scatter_about(arg_keys[8], (R, FF), (4 * R) ** -0.5, 0.25, ((0, 8), (1, 32)), jnp.float32)
    up_b = scatter_about(arg_keys[9], (R, FF), (4 * R) ** -0.5, 0.25, ((0, 8), (1, 32)), jnp.float32)
    down_a_t = scatter_about(arg_keys[10], (R, FF), FF ** -0.5, 0.03125, ((0, 8), (1, 32)), jnp.float32)
    return dict(tokens=tokens, out_grad=out_grad, gate_w=gate_w, up_w=up_w, down_w=down_w, gate_a=gate_a, up_a=up_a, down_b_t=down_b_t, gate_b=gate_b, up_b=up_b, down_a_t=down_a_t)


def contract_last(left, right, precision_kind):
    return lax.dot_general(left, right, (((1,), (1,)), ((), ())), precision=precision_kind, preferred_element_type=jnp.float32)


def contract_first(left, right):
    return lax.dot_general(left, right, (((0,), (0,)), ((), ())), precision=lax.Precision.HIGHEST, preferred_element_type=jnp.float32)


def reference(tokens, out_grad, gate_w, up_w, down_w, gate_a, up_a, down_b_t, gate_b, up_b, down_a_t):
    highest = lax.Precision.HIGHEST
    x_float = tokens.astype(jnp.float32)
    dy_float = out_grad.astype(jnp.float32)
    xa_gate = jnp.dot(x_float, gate_a, precision=highest, preferred_element_type=jnp.float32)
    xa_up = jnp.dot(x_float, up_a, precision=highest, preferred_element_type=jnp.float32)
    dy_rank = jnp.dot(dy_float, down_b_t, precision=highest, preferred_element_type=jnp.float32)
    gate_pre = jnp.dot(tokens, gate_w, preferred_element_type=jnp.float32) + jnp.dot(xa_gate, gate_b, precision=highest, preferred_element_type=jnp.float32)
    up_pre = jnp.dot(tokens, up_w, preferred_element_type=jnp.float32) + jnp.dot(xa_up, up_b, precision=highest, preferred_element_type=jnp.float32)
    grad_hidden = contract_last(out_grad, down_w, None) + jnp.dot(dy_rank, down_a_t, precision=highest, preferred_element_type=jnp.float32)
    sigma = jax.nn.sigmoid(gate_pre)
    hidden = (gate_pre * sigma * up_pre).astype(jnp.bfloat16)
    d_gate = (grad_hidden * up_pre * sigma * (1.0 + gate_pre * (1.0 - sigma))).astype(jnp.bfloat16)
    d_up = (grad_hidden * gate_pre * sigma).astype(jnp.bfloat16)
    d_gate_float = d_gate.astype(jnp.float32)
    d_up_float = d_up.astype(jnp.float32)
    hidden_float = hidden.astype(jnp.float32)
    g_rank = contract_last(d_gate_float, gate_b, highest)
    u_rank = contract_last(d_up_float, up_b, highest)
    h_rank = contract_last(hidden_float, down_a_t, highest)
    grad_sum = contract_last(d_gate, gate_w, None) + contract_last(d_up, up_w, None)
    grad_tokens = grad_sum + contract_last(g_rank, gate_a, highest) + contract_last(u_rank, up_a, highest)
    grad_gate_a = contract_first(x_float, g_rank)
    grad_up_a = contract_first(x_float, u_rank)
    grad_gate_b = contract_first(xa_gate, d_gate_float)
    grad_up_b = contract_first(xa_up, d_up_float)
    grad_down_a_t = contract_first(dy_rank, hidden_float)
    grad_down_b_t = contract_first(dy_float, h_rank)
    return (grad_tokens, grad_gate_a, grad_up_a, grad_gate_b, grad_up_b, grad_down_a_t, grad_down_b_t)
```

```python
import jax
import jax.numpy as jnp
from jax import lax
from jax.sharding import Mesh, PartitionSpec as P

ROW = ("x", "zl")
COL = ("zh", "y", "c")
NX, NZL, NZH, NY, NC = 4, 2, 4, 4, 2
NROW = NX * NZL
CHUNKS = 1
F32, F16, BF16 = jnp.float32, jnp.float16, jnp.bfloat16
F16_TOP = 32768.0
TINY = 1e-30


def split(a):
    hi = lax.reduce_precision(a, 8, 7)
    return hi.astype(BF16), (a - hi).astype(BF16)


def dot(a, b, dims=((1,), (0,))):
    return lax.dot_general(a, b, (dims, ((), ())), preferred_element_type=F32)


def dot3(a, b, dims=((1,), (0,))):
    ah, al = split(a)
    bh, bl = split(b)
    return dot(ah, bh, dims) + (dot(ah, bl, dims) + dot(al, bh, dims))


def shift(a, axis, n, s):
    return lax.ppermute(a, axis, [(j, (j - s) % n) for j in range(n)])


def in_order(blocks, axis, n):
    doubled = jnp.concatenate(blocks + blocks[:-1], axis=0)
    rows = blocks[0].shape[0]
    start = ((n - lax.axis_index(axis)) % n) * rows
    return lax.dynamic_slice_in_dim(doubled, start, n * rows, 0)


def gather(a, axis, n):
    order = (1, 3, 2) if n == 4 else (1,)
    got = {0: a}
    for s in order:
        got[s] = shift(a, axis, n, s)
    return in_order([got[s] for s in range(n)], axis, n)


def spread(a, axis, n):
    wide = jnp.broadcast_to(a[None], (n,) + a.shape).reshape((n * a.shape[0],) + a.shape[1:])
    return lax.all_to_all(wide, axis, split_axis=0, concat_axis=0, tiled=True)


def block(a, axis, n, s):
    rows = a.shape[0] // n
    return lax.dynamic_slice_in_dim(a, ((lax.axis_index(axis) + s) % n) * rows, rows, 0)


def reduce_to_own(a, axis, n, kind):
    total = block(a, axis, n, 0)
    order = (1, 3, 2) if n == 4 else (1,)
    for s in order:
        sent = block(a, axis, n, s).astype(kind)
        total = total + lax.ppermute(sent, axis, [(j, (j + s) % n) for j in range(n)]).astype(F32)
    return total


def sum_all(a, axis, n):
    total = a
    for s in (1, 3, 2) if n == 4 else (1,):
        total = total + shift(a, axis, n, s)
    return total


def top(a):
    return jnp.max(jnp.abs(a)).astype(F32)


def body(tokens, out_grad, gate_w, up_w, down_w, gate_a, up_a, down_b_t, gate_b, up_b, down_a_t):
    own = tokens.shape[0] // CHUNKS
    width = tokens.shape[1]
    hidden_units = gate_w.shape[1]
    rank = gate_a.shape[1]
    rank_share = gate_b.shape[0]

    def panel_of(k):
        rows = slice(k * own, (k + 1) * own)
        both = jnp.concatenate([tokens[rows], out_grad[rows]], axis=1)
        for axis, n in (("zh", NZH), ("y", NY), ("c", NC)):
            both = gather(both, axis, n)
        return both

    panels = [panel_of(k) for k in range(CHUNKS)]

    a_own = jnp.concatenate([gate_a, up_a, down_b_t], axis=1)
    a_top = jnp.maximum(top(a_own), TINY)
    a_exp = jnp.ceil(jnp.log2(a_top))
    a_scaled = (a_own * jnp.exp2(14.0 - a_exp)).astype(F16)
    a_pack = jnp.concatenate([a_scaled, jnp.full((8, a_own.shape[1]), a_exp, F16)], axis=0)
    for axis, n in (("zh", NZH), ("y", NY), ("c", NC)):
        a_pack = spread(a_pack, axis, n)
    own_features = gate_a.shape[0]
    a_pack = a_pack.reshape(NC, NY, NZH, own_features + 8, 3 * rank).transpose(2, 1, 0, 3, 4)
    a_scale = jnp.exp2(a_pack[..., own_features : own_features + 1, :].astype(F32) - 14.0)
    a_all = (a_pack[..., :own_features, :].astype(F32) * a_scale).reshape(width, 3 * rank)
    a_hi, a_lo = split(a_all)

    b_own = jnp.concatenate([gate_b, up_b, down_a_t], axis=0)
    b_all = spread(b_own, ROW, NROW).reshape(NROW, 3, rank_share, hidden_units)
    b_gate, b_up, a_down = (b_all[:, i].reshape(rank, hidden_units) for i in range(3))

    w_top = [top(gate_w), top(up_w), top(down_w)]
    b_top = [top(b_gate), top(b_up), top(a_down)]

    kept = []
    for k in range(CHUNKS):
        panel = panels[k]
        x, dy = panel[:, :width], panel[:, width:]
        x_top, dy_top = top(x), top(dy)
        xa = dot(x, a_hi[:, : 2 * rank]) + dot(x, a_lo[:, : 2 * rank])
        dya = dot(dy, a_hi[:, 2 * rank :]) + dot(dy, a_lo[:, 2 * rank :])
        ranks = (xa[:, :rank], xa[:, rank:], dya)
        tops = (x_top, x_top, dy_top)
        bounds = jnp.stack(
            [
                1.01 * (width * tops[i] * w_top[i] + rank * top(ranks[i]) * b_top[i]) + TINY
                for i in range(3)
            ]
        )
        bound_pack = jnp.broadcast_to(
            jnp.pad(bounds / F16_TOP, (0, 125))[None, None], (NROW, 8, 128)
        ).reshape(NROW * 8, 128)
        bound_all = lax.all_to_all(bound_pack, ROW, split_axis=0, concat_axis=0, tiled=True)
        unscale = bound_all.reshape(NROW, 8, 128)[:, 0, :3]
        scale = F16_TOP / bounds
        part_gate = dot(x, gate_w) + dot3(ranks[0], b_gate)
        part_up = dot(x, up_w) + dot3(ranks[1], b_up)
        part_down = dot(dy, down_w, ((1,), (1,))) + dot3(ranks[2], a_down)
        parts = jnp.concatenate(
            [
                (part_gate * scale[0]).astype(F16),
                (part_up * scale[1]).astype(F16),
                (part_down * scale[2]).astype(F16),
            ],
            axis=1,
        )
        got = lax.all_to_all(parts, ROW, split_axis=0, concat_axis=0, tiled=True)
        got = got.reshape(NROW, -1, 3, hidden_units)
        gate_pre, up_pre, grad_hidden = (
            sum(got[s, :, i].astype(F32) * unscale[s, i] for s in range(NROW)) for i in range(3)
        )
        sigma = jax.nn.sigmoid(gate_pre)
        hidden = (gate_pre * sigma * up_pre).astype(BF16)
        d_gate = (grad_hidden * up_pre * sigma * (1.0 + gate_pre * (1.0 - sigma))).astype(BF16)
        d_up = (grad_hidden * gate_pre * sigma).astype(BF16)
        kept.append((panel, ranks, hidden, d_gate, d_up))

    def rank_sum(i, b):
        bh, bl = split(b)
        d = jnp.concatenate([c[i] for c in kept], axis=0)
        return dot(d, bh, ((1,), (1,))) + dot(d, bl, ((1,), (1,)))

    g_part = jnp.concatenate(
        [rank_sum(3, b_gate), rank_sum(4, b_up), rank_sum(2, a_down)], axis=1
    )
    for axis, n in (("c", NC), ("y", NY), ("zh", NZH)):
        g_part = sum_all(g_part, axis, n)

    grads = []
    for k in range(CHUNKS):
        d_both = jnp.concatenate([kept[k][3], kept[k][4]], axis=1)
        d_all = spread(d_both, ROW, NROW)
        d_gate, d_up = d_all[:, :hidden_units], d_all[:, hidden_units:]
        part = dot(d_gate, gate_w, ((1,), (1,))) + dot(d_up, up_w, ((1,), (1,)))
        part = reduce_to_own(part, "c", NC, F32)
        part = reduce_to_own(part, "y", NY, BF16)
        part = reduce_to_own(part, "zh", NZH, F32)
        grads.append((part, d_gate, d_up))

    g_all = spread(g_part, ROW, NROW)
    h_own = jnp.concatenate([c[2] for c in kept], axis=0)
    h_all = spread(h_own, ROW, NROW)
    per = g_part.shape[0] // CHUNKS

    def chunk_rows(a, k):
        return a.reshape(NROW, CHUNKS, per, a.shape[1])[:, k].reshape(NROW * per, a.shape[1])

    rank_t = jnp.concatenate(
        [jnp.concatenate([c[1][i] for i in range(3)], axis=1) for c in kept], axis=0
    ).T
    rank_t = rank_t.reshape(3, NROW, rank_share, -1).transpose(1, 0, 2, 3)
    rank_t = rank_t.reshape(NROW * 3 * rank_share, -1)
    rank_got = lax.all_to_all(rank_t, ROW, split_axis=0, concat_axis=0, tiled=True)
    rank_own = rank_got.reshape(NROW, 3, rank_share, -1).sum(0)

    zh, y, c = (lax.axis_index(a) for a in ("zh", "y", "c"))
    own_start = ((c * NY + y) * NZH + zh) * own
    feature_start = ((zh * NY + y) * NC + c) * own_features
    g_all = [chunk_rows(g_all, k) for k in range(CHUNKS)]
    grad_tokens = []
    for k in range(CHUNKS):
        g_own = lax.dynamic_slice_in_dim(g_all[k], own_start, own, 0)[:, : 2 * rank]
        grad_tokens.append(grads[k][0] + dot3(g_own, a_all[:, : 2 * rank], ((1,), (1,))))
    grad_tokens = jnp.concatenate(grad_tokens, axis=0)

    panel = jnp.concatenate([c[0] for c in kept], axis=0)
    x_own = lax.dynamic_slice_in_dim(panel, feature_start, own_features, 1)
    dy_own = lax.dynamic_slice_in_dim(panel, width + feature_start, own_features, 1)
    g_cat = jnp.concatenate(g_all, axis=0)
    gh, gl = split(g_cat)

    def first(a, b):
        return dot(a, b, ((0,), (0,)))

    grad_x = first(x_own, gh[:, : 2 * rank]) + first(x_own, gl[:, : 2 * rank])
    grad_down_b_t = first(dy_own, gh[:, 2 * rank :]) + first(dy_own, gl[:, 2 * rank :])

    rh, rl = split(rank_own)
    d_gate = jnp.concatenate([g[1] for g in grads], axis=0)
    d_up = jnp.concatenate([g[2] for g in grads], axis=0)
    hidden = jnp.concatenate([chunk_rows(h_all, k) for k in range(CHUNKS)], axis=0)
    grad_b = [dot(rh[i], d) + dot(rl[i], d) for i, d in enumerate((d_gate, d_up, hidden))]
    return (
        grad_tokens,
        grad_x[:, :rank],
        grad_x[:, rank:],
        grad_b[0],
        grad_b[1],
        grad_b[2],
        grad_down_b_t,
    )


def solution(mesh):
    fine = Mesh(mesh.devices.reshape(NX, NZL, NZH, NY, NC), ROW + COL)
    tiled = P(COL, ROW)
    weight = P(ROW, COL)
    factor = P(ROW + COL, None)
    return jax.shard_map(
        body,
        mesh=fine,
        in_specs=(tiled, tiled, weight, weight, tiled, factor, factor, factor, weight, weight, weight),
        out_specs=(tiled, factor, factor, weight, weight, weight, factor),
        check_vma=False,
    )
```

```python
import jax
import jax.numpy as jnp
from jax import lax
from jax.experimental import pallas as pl
from jax.experimental.pallas import tpu as pltpu
from jax.sharding import Mesh, PartitionSpec as P

ROW = ("x", "zl")
COL = ("zh", "y", "c")
NX, NZL, NZH, NY, NC = 4, 2, 4, 4, 2
NROW = NX * NZL
F32, F16, BF16 = jnp.float32, jnp.float16, jnp.bfloat16
F16_TOP = 32768.0
TINY = 1e-30
SHIFTS = (1, 3, 2)
VMEM = pl.BlockSpec(memory_space=pltpu.VMEM)
SMEM = pl.BlockSpec(memory_space=pltpu.SMEM)
ANY = pl.BlockSpec(memory_space=pl.ANY)
PARAMS = pltpu.CompilerParams(vmem_limit_bytes=48 * 1024 * 1024)


def split(a):
    hi = a.astype(BF16)
    return hi, (a - hi.astype(F32)).astype(BF16)


def dot(a, b, dims=((1,), (0,))):
    return lax.dot_general(a, b, (dims, ((), ())), preferred_element_type=F32)


def dot2(a, b, dims=((1,), (0,))):
    bh, bl = split(b)
    return dot(a, bh, dims) + dot(a, bl, dims)


def dot3(a, b, dims=((1,), (0,))):
    ah, al = split(a)
    bh, bl = split(b)
    return dot(ah, bh, dims) + (dot(ah, bl, dims) + dot(al, bh, dims))


def shape(dims, kind):
    return jax.ShapeDtypeStruct(dims, kind)


def from_next(a, axis, n, s):
    return lax.ppermute(a, axis, [(j, (j - s) % n) for j in range(n)])


def to_next(a, axis, n, s):
    return lax.ppermute(a, axis, [(j, (j + s) % n) for j in range(n)])


def exchange(wide, axis):
    return lax.all_to_all(wide, axis, split_axis=0, concat_axis=0)


def cost(flops, *arrays):
    moved = sum(a.size * a.dtype.itemsize for a in arrays)
    return pl.CostEstimate(flops=flops, bytes_accessed=moved, transcendentals=0)


def pack(tokens, out_grad, *factors):
    own, width = out_grad.shape
    own_features, rank = factors[0].shape
    ranks = rank * len(factors)
    groups = own_features // own

    def kernel(x, dy, *refs):
        out = refs[-1]
        out[:, :width] = x[...]
        out[:, width : 2 * width] = dy[...]
        halves = [split(ref[...]) for ref in refs[:-1]]
        order = [h[0] for h in halves[:-1]] + [h[1] for h in halves[:-1]] + list(halves[-1])
        for k in range(groups):
            for i, value in enumerate(order):
                at = 2 * width + k * 2 * ranks + i * rank
                out[:, at : at + rank] = value[k * own : (k + 1) * own]

    return pl.pallas_call(
        kernel,
        out_shape=shape((own, 2 * width + groups * 2 * ranks), BF16),
        in_specs=[VMEM] * (2 + len(factors)),
        out_specs=VMEM,
    )(tokens, out_grad, *factors)


def join_rows(here, cut, *parts):
    rows, lanes = parts[0].shape

    def kernel(here, *refs):
        left, right = refs[-2:]
        for s, ref in enumerate(refs[:-2]):
            at = pl.multiple_of(lax.rem(here[0] + s, len(parts)) * rows, rows)
            left[pl.ds(at, rows), :] = ref[:, :cut]
            right[pl.ds(at, rows), :] = ref[:, cut:]

    return pl.pallas_call(
        kernel,
        out_shape=(
            shape((rows * len(parts), cut), parts[0].dtype),
            shape((rows * len(parts), lanes - cut), parts[0].dtype),
        ),
        in_specs=[SMEM] + [VMEM] * len(parts),
        out_specs=(VMEM, VMEM),
    )(here, *parts)


def panel_moves(place, pieces, first, size, target, sems):
    y, c = place[1], place[2]
    moves = []
    for dc in range(NC):
        for d in range(NY):
            block = lax.rem(c + dc, NC) * NY + lax.rem(y + d, NY)
            piece = pieces[dc * NY + d]
            rows = piece.shape[0]
            moves.append(
                pltpu.make_async_copy(
                    piece.at[:, pl.ds(first, size)],
                    target.at[pl.ds(pl.multiple_of(block * rows, rows), rows)],
                    sems.at[dc * NY + d],
                )
            )
    return moves


def scaled(part, at, size, values, index, exponents):
    rows = part.shape[0]
    step = rows // 4
    top = jnp.float32(TINY)
    for k in range(0, rows, step):
        value = values(slice(k, k + step))
        part[k : k + step, at : at + size] = value
        top = jnp.maximum(top, jnp.max(jnp.abs(value)))
    exponent = jnp.ceil(jnp.log2(jnp.full((1, 128), top, F32))) - 15.0
    scale = jnp.exp2(-exponent)[:, :1]
    for k in range(0, rows, step):
        part[k : k + step, at : at + size] = part[k : k + step, at : at + size] * scale
    lane = lax.broadcasted_iota(jnp.int32, (1, 128), 1)
    return jnp.where(lane // 16 == index, exponent, exponents)


def forward_x(place, pieces, gate_w, up_w):
    quarter = pieces[0].shape[0]
    width, units = gate_w.shape
    rows = quarter * NY * NC

    def kernel(place, *refs):
        piece = refs[:8]
        gate, up, part_out, x_out, exponents_out = refs[8:13]
        part, x, w_gate, w_up, sem_x, sem_w, sem_o = refs[13:]
        moves = panel_moves(place, piece, 0, width, x, sem_x)
        load = [
            pltpu.make_async_copy(a, b, sem_w.at[i])
            for i, (a, b) in enumerate(((gate, w_gate), (up, w_up)))
        ]
        store = [
            pltpu.make_async_copy(
                part.at[:, pl.ds(i * units, units)],
                part_out.at[:, pl.ds(i * units, units)],
                sem_o.at[i],
            )
            for i in range(2)
        ]
        store_x = pltpu.make_async_copy(x, x_out, sem_o.at[2])
        for copy in moves + load:
            copy.start()
        for copy in moves + load[:1]:
            copy.wait()
        store_x.start()
        exponents = jnp.zeros((1, 128), F32)
        exponents = scaled(part, 0, units, lambda at: dot(x[at, :], w_gate[...]), 0, exponents)
        store[0].start()
        load[1].wait()
        exponents = scaled(part, units, units, lambda at: dot(x[at, :], w_up[...]), 1, exponents)
        store[1].start()
        exponents_out[...] = jnp.broadcast_to(exponents, (8, 128))
        for copy in store + [store_x]:
            copy.wait()

    return pl.pallas_call(
        kernel,
        out_shape=(
            shape((rows, 2 * units), F32),
            shape((rows, width), BF16),
            shape((8, 128), F32),
        ),
        in_specs=[SMEM] + [ANY] * 10,
        out_specs=(ANY, ANY, VMEM),
        scratch_shapes=[
            pltpu.VMEM((rows, 2 * units), F32),
            pltpu.VMEM((rows, width), BF16),
            pltpu.VMEM(gate_w.shape, BF16),
            pltpu.VMEM(up_w.shape, BF16),
            pltpu.SemaphoreType.DMA((8,)),
            pltpu.SemaphoreType.DMA((2,)),
            pltpu.SemaphoreType.DMA((3,)),
        ],
        compiler_params=PARAMS,
        cost_estimate=cost(12 * rows * width * units, gate_w, up_w),
    )(place, *pieces, gate_w, up_w)


def forward_dy(place, pieces, x, down_w, exponents, ranks, own_features):
    quarter, lanes = pieces[0].shape
    own = quarter // NZH
    rows, width = x.shape
    units = down_w.shape[0]
    rank = ranks // 3
    groups = own_features // own

    def kernel(place, *refs):
        piece = refs[:8]
        x_in, down, exponents_in, part, dy_out, factors = refs[8:14]
        x, dy, packed, w_down, sem_dy, sem_a, sem_w, sem_o = refs[14:]
        move_dy = panel_moves(place, piece, 0, width, dy, sem_dy)
        move_a = panel_moves(place, piece, width, lanes - width, packed, sem_a)
        load = [
            pltpu.make_async_copy(down, w_down, sem_w.at[0]),
            pltpu.make_async_copy(x_in, x, sem_w.at[1]),
        ]
        store_dy = pltpu.make_async_copy(dy, dy_out, sem_o)
        for copy in move_dy + load[:1] + move_a + load[1:]:
            copy.start()
        for copy in move_dy + load[:1]:
            copy.wait()
        store_dy.start()
        exponents = exponents_in[0:1, :]
        exponents = scaled(
            part, 0, units, lambda at: dot(dy[at, :], w_down[...], ((1,), (1,))), 2, exponents
        )
        for copy in move_a + load[1:]:
            copy.wait()
        for c in range(NC):
            for y in range(NY):
                for zh in range(NZH):
                    to = ((zh * NY + y) * NC + c) * own_features
                    at = ((c * NY + y) * NZH + zh) * own
                    for k in range(groups):
                        factors[to + k * own : to + (k + 1) * own, :] = packed[
                            at : at + own, k * 2 * ranks : (k + 1) * 2 * ranks
                        ]
        xa = dot(x[...], factors[:, : 2 * rank]) + dot(x[...], factors[:, 2 * rank : 4 * rank])
        dya = dot(dy[...], factors[:, 4 * rank :])
        dya = dya[:, :rank] + dya[:, rank:]
        values = (xa[:, :rank], xa[:, rank:], dya)
        for i, value in enumerate(values):
            exponents = scaled(
                part, units + i * rank, rank, lambda at: value[at, :], 3 + i, exponents
            )
        part[:, units + ranks :] = jnp.broadcast_to(exponents, (rows, 128))
        store_dy.wait()

    return pl.pallas_call(
        kernel,
        out_shape=(
            shape((rows, units + ranks + 128), F32),
            shape((rows, width), BF16),
            shape((width, 2 * ranks), BF16),
        ),
        in_specs=[SMEM] + [ANY] * 10 + [VMEM],
        out_specs=(VMEM, ANY, VMEM),
        scratch_shapes=[
            pltpu.VMEM((rows, width), BF16),
            pltpu.VMEM((rows, width), BF16),
            pltpu.VMEM((rows, lanes - width), BF16),
            pltpu.VMEM(down_w.shape, BF16),
            pltpu.SemaphoreType.DMA((8,)),
            pltpu.SemaphoreType.DMA((8,)),
            pltpu.SemaphoreType.DMA((2,)),
            pltpu.SemaphoreType.DMA,
        ],
        compiler_params=PARAMS,
        cost_estimate=cost(12 * rows * width * units, down_w, x),
    )(place, *pieces, x, down_w, exponents)


def swiglu_back(first, second, b_parts):
    per, lanes = second.shape[1:]
    share, units = b_parts.shape[1] // 3, b_parts.shape[2]
    rank = share * NROW
    ranks = 3 * rank
    sizes = [units] * 3 + [rank] * 3
    starts = [0, units, 0, units, units + rank, units + 2 * rank]

    def kernel(first, second, b_parts, wide, g_out, factor_out, b):
        for i in range(3):
            for r in range(NROW):
                b[i, r * share : (r + 1) * share, :] = b_parts[r, i * share : (i + 1) * share, :]
        scales = [jnp.exp2(second[r, 0:1, lanes - 128 :]) for r in range(NROW)]

        def total(i):
            value = 0.0
            sums = first if i < 2 else second
            for r in range(NROW):
                part = sums[r, :, starts[i] : starts[i] + sizes[i]]
                value = value + part * scales[r][:, 16 * i : 16 * i + 1]
            return value

        products = [total(3 + i) for i in range(3)]
        gate_pre, up_pre, grad_hidden = (total(i) + dot3(products[i], b[i]) for i in range(3))
        sigma = 1.0 / (1.0 + jnp.exp(-gate_pre))
        hidden = (gate_pre * sigma * up_pre).astype(BF16)
        d_gate = (grad_hidden * up_pre * sigma * (1.0 + gate_pre * (1.0 - sigma))).astype(BF16)
        d_up = (grad_hidden * gate_pre * sigma).astype(BF16)
        for r in range(NROW):
            wide[r, :, :units] = d_gate
            wide[r, :, units:] = d_up
        for i, d in enumerate((d_gate, d_up, hidden)):
            g_out[:, i * rank : (i + 1) * rank] = dot2(d, b[i], ((1,), (1,)))
            hi, lo = split(products[i].T)
            grad = dot(hi, d) + dot(lo, d)
            for r in range(NROW):
                factor_out[r, i * share : (i + 1) * share, :] = grad[
                    r * share : (r + 1) * share
                ].astype(BF16)

    return pl.pallas_call(
        kernel,
        out_shape=(
            shape((NROW, per, 2 * units), BF16),
            shape((per, ranks), F32),
            shape(b_parts.shape, BF16),
        ),
        in_specs=[VMEM] * 3,
        out_specs=(VMEM,) * 3,
        scratch_shapes=[pltpu.VMEM((3, rank, units), F32)],
        compiler_params=PARAMS,
        cost_estimate=cost(24 * per * rank * units, first, second),
    )(first, second, b_parts)


def backward(which, d_all, gate_w, up_w):
    half = d_all.shape[0] // NC
    width, units = gate_w.shape

    def kernel(which, d, gate, up, out):
        at = pl.ds(pl.multiple_of(which[0] * half, half), half)
        out[...] = dot(d[at, :units], gate[...], ((1,), (1,))) + dot(
            d[at, units:], up[...], ((1,), (1,))
        )

    return pl.pallas_call(
        kernel,
        out_shape=shape((half, width), F32),
        in_specs=[SMEM] + [VMEM] * 3,
        out_specs=VMEM,
        compiler_params=PARAMS,
        cost_estimate=cost(4 * half * width * units, gate_w, up_w),
    )(which, d_all, gate_w, up_w)


def add_and_cut(here, kind, *parts):
    rows, width = parts[0].shape
    block = rows // 4

    def kernel(here, *refs):
        ins, outs = refs[: len(parts)], refs[len(parts) :]
        for s, out in zip((0,) + SHIFTS, outs):
            at = pl.ds(pl.multiple_of(lax.rem(here[0] + s, 4) * block, block), block)
            total = ins[0][at, :].astype(F32)
            for ref in ins[1:]:
                total = total + ref[at, :].astype(F32)
            out[...] = total.astype(out.dtype)

    return pl.pallas_call(
        kernel,
        out_shape=(shape((block, width), F32),) + (shape((block, width), kind),) * 3,
        in_specs=[SMEM] + [VMEM] * len(parts),
        out_specs=(VMEM,) * 4,
        compiler_params=PARAMS,
    )(here, *parts)


def merge(factor_parts, g):
    share, units = factor_parts.shape[1:]
    per, ranks = g.shape

    def kernel(parts, g, out):
        hi, lo = split(g[...])
        for r in range(NROW):
            out[r, :share, :] = parts[r]
            out[r, share:, :ranks] = hi
            out[r, share:, ranks : 2 * ranks] = lo
            out[r, share:, 2 * ranks :] = jnp.zeros((per, units - 2 * ranks), BF16)

    return pl.pallas_call(
        kernel,
        out_shape=shape((NROW, share + per, units), BF16),
        in_specs=[VMEM] * 2,
        out_specs=VMEM,
    )(factor_parts, g)


def select(place, x, dy, own_features):
    rows, width = x.shape

    def kernel(place, x, dy, out):
        y, c = place[1], place[2]
        row = lax.broadcasted_iota(jnp.int32, (own_features, width), 0)
        lane = lax.broadcasted_iota(jnp.int32, (own_features, width), 1)
        for zh in range(NZH):
            start = ((zh * NY + y) * NC + c) * own_features
            pick = jnp.where(lane == row + start, 1.0, 0.0).astype(BF16)
            for i, panel in enumerate((x, dy)):
                at = (i * NZH + zh) * own_features
                out[at : at + own_features, :] = dot(pick, panel[...], ((1,), (1,))).astype(BF16)

    return pl.pallas_call(
        kernel,
        out_shape=shape((2 * NZH * own_features, rows), BF16),
        in_specs=[SMEM, VMEM, VMEM],
        out_specs=VMEM,
        compiler_params=PARAMS,
        cost_estimate=cost(4 * NZH * own_features * rows * width, x, dy),
    )(place, x, dy)


def rank_grads(place, selected, merged, factors, ranks):
    features = selected.shape[0] // 2
    rows = selected.shape[1]
    per = rows // NROW
    rank = ranks // 3
    share = merged.shape[1] - per
    width = factors.shape[0]

    def kernel(place, selected, merged, factors, grads, adapter, g):
        for r in range(NROW):
            g[r * per : (r + 1) * per, :] = merged[r, share:, : 2 * ranks]
        hi, lo = g[:, :ranks], g[:, ranks:]
        xs, dys = selected[:features, :], selected[features:, :]
        grads[:, : 2 * rank] = dot(xs, hi[:, : 2 * rank]) + dot(xs, lo[:, : 2 * rank])
        grads[:, 2 * rank :] = dot(dys, hi[:, 2 * rank :]) + dot(dys, lo[:, 2 * rank :])
        block = place[2] * NY + place[1]
        own = g[pl.ds(pl.multiple_of(block * per, per), per), :]
        gh, gl = own[:, : 2 * rank], own[:, ranks : ranks + 2 * rank]
        ah, al = factors[:, : 2 * rank], factors[:, 2 * rank : 4 * rank]
        last = ((1,), (1,))
        adapter[...] = dot(gh, ah, last) + (dot(gl, ah, last) + dot(gh, al, last))

    return pl.pallas_call(
        kernel,
        out_shape=(shape((features, ranks), F32), shape((per, width), F32)),
        in_specs=[SMEM] + [VMEM] * 3,
        out_specs=(VMEM, VMEM),
        scratch_shapes=[pltpu.VMEM((rows, 2 * ranks), BF16)],
        compiler_params=PARAMS,
    )(place, selected, merged, factors)


def cut_last(here, grads, *parts):
    rows, width = parts[0].shape
    block = rows // NZH
    features = grads.shape[0] // NZH
    ranks = grads.shape[1]
    groups = features // block

    def kernel(here, grads, *refs):
        ins, outs = refs[: len(parts)], refs[len(parts) :]
        for s, out in zip((0,) + SHIFTS, outs):
            to = lax.rem(here[0] + s, NZH)
            at = pl.ds(pl.multiple_of(to * block, block), block)
            total = ins[0][at, :].astype(F32)
            for ref in ins[1:]:
                total = total + ref[at, :].astype(F32)
            out[:, :width] = total
            for k in range(groups):
                at = pl.ds(pl.multiple_of(to * features + k * block, block), block)
                out[:, width + k * ranks : width + (k + 1) * ranks] = grads[at, :]

    return pl.pallas_call(
        kernel,
        out_shape=(shape((block, width + groups * ranks), F32),) * 4,
        in_specs=[SMEM] + [VMEM] * (1 + len(parts)),
        out_specs=(VMEM,) * 4,
        compiler_params=PARAMS,
    )(here, grads, *parts)


def finish(width, rank, *parts):
    own, lanes = parts[0].shape
    ranks = 3 * rank
    groups = (lanes - width) // ranks

    def kernel(*refs):
        ins, (tokens, *factors) = refs[:4], refs[4:]
        total = (ins[0][...] + ins[1][...]) + (ins[2][...] + ins[3][...])
        tokens[...] = total[:, :width]
        for k in range(groups):
            for i, out in enumerate(factors):
                at = width + k * ranks + i * rank
                out[k * own : (k + 1) * own, :] = total[:, at : at + rank]

    return pl.pallas_call(
        kernel,
        out_shape=(shape((own, width), F32),) + (shape((own * groups, rank), F32),) * 3,
        in_specs=[VMEM] * 4,
        out_specs=(VMEM,) * 4,
    )(*parts)


def after(value, *others):
    return lax.optimization_barrier((value,) + others)[0]


def body(tokens, out_grad, gate_w, up_w, down_w, gate_a, up_a, down_b_t, gate_b, up_b, down_a_t):
    own, width = tokens.shape
    units = gate_w.shape[1]
    own_features, rank = gate_a.shape
    zh, y, c = (lax.axis_index(a) for a in COL)
    row = lax.axis_index(ROW)
    place = jnp.stack([zh, y, c, row]).astype(jnp.int32)

    at_zh, at_y, at_c, at_other = (
        v.reshape(1).astype(jnp.int32) for v in (zh, y, c, (c + 1) % NC)
    )
    ranks = 3 * rank

    mine = pack(tokens, out_grad, gate_a, up_a, down_b_t)
    got = {0: mine}
    for s in SHIFTS:
        got[s] = from_next(mine, "zh", NZH, s)
    near, late = join_rows(at_zh, width, *[got[s] for s in range(NZH)])

    def from_y(a):
        got = {0: a}
        for s in SHIFTS:
            got[s] = from_next(a, "y", NY, s)
        return [got[s] for s in range(NY)]

    def with_core(pieces):
        return pieces + [from_next(p, "c", NC, 1) for p in pieces]

    b_own = after(jnp.concatenate([gate_b, up_b, down_a_t], axis=0), near)
    b_parts = exchange(jnp.broadcast_to(b_own[None], (NROW,) + b_own.shape), ROW)
    pieces = from_y(near)
    late_pieces = from_y(after(late, pieces[2]))
    pieces = with_core(pieces)

    def sums(part):
        sent = part.astype(F16).reshape(NROW, rows // NROW, part.shape[1])
        return exchange(sent, ROW).astype(F32)

    part_x, x, exponents = forward_x(place, pieces, gate_w, up_w)
    rows = x.shape[0]
    part_x, b_parts, *late_pieces = lax.optimization_barrier((part_x, b_parts, *late_pieces))
    part_dy, dy, factors = forward_dy(
        place, with_core(late_pieces), x, down_w, exponents, ranks, own_features
    )
    sums_x = sums(part_x)
    sums_x, part_dy = lax.optimization_barrier((sums_x, part_dy))
    selected = select(place, x, dy, own_features)
    wide, g, factor_parts = swiglu_back(sums_x, sums(part_dy), b_parts)

    d_all = exchange(wide, ROW).reshape(rows, 2 * units)

    g = g + from_next(g, "c", NC, 1)
    g = g + sum(from_next(g, "y", NY, s) for s in SHIFTS)
    merged = merge(factor_parts, g)
    d_all, merged, selected = lax.optimization_barrier((d_all, merged, selected))
    merged = exchange(merged, ROW)

    sent = backward(at_other, d_all, gate_w, up_w)
    other = from_next(sent, "c", NC, 1)
    kept = backward(at_c, after(d_all, sent), gate_w, up_w)
    kept, *sends = add_and_cut(at_y, BF16, kept, other)
    others = [to_next(a, "y", NY, s) for s, a in zip(SHIFTS, sends)]

    grads, adapter = rank_grads(place, selected, merged, factors, ranks)
    kept, *sends = cut_last(at_zh, grads, kept, *others, adapter)
    others = [to_next(a, "zh", NZH, s) for s, a in zip(SHIFTS, sends)]
    grad_tokens, grad_gate_a, grad_up_a, grad_down_b_t = finish(width, rank, kept, *others)

    share = gate_b.shape[0]
    factor_grads = merged[:, : 3 * share].astype(F32).sum(0)
    grad_b = [factor_grads[i * share : (i + 1) * share] for i in range(3)]
    return (grad_tokens, grad_gate_a, grad_up_a, *grad_b, grad_down_b_t)


def solution(mesh):
    fine = Mesh(mesh.devices.reshape(NX, NZL, NZH, NY, NC), ROW + COL)
    tiled = P(COL, ROW)
    weight = P(ROW, COL)
    factor = P(ROW + COL, None)
    return jax.shard_map(
        body,
        mesh=fine,
        in_specs=(tiled, tiled, weight, weight, tiled, factor, factor, factor, weight, weight, weight),
        out_specs=(tiled, factor, factor, weight, weight, weight, factor),
        check_vma=False,
    )
```

```python
import jax
import jax.numpy as jnp
from jax import lax
from jax.experimental import pallas as pl
from jax.experimental.pallas import tpu as pltpu
from jax.sharding import Mesh, PartitionSpec as P

ROW = ("x", "zl")
COL = ("zh", "y", "c")
NX, NZL, NZH, NY, NC = 4, 2, 4, 4, 2
NROW = NX * NZL
F32, F16, BF16 = jnp.float32, jnp.float16, jnp.bfloat16
F16_TOP = 32768.0
TINY = 1e-30
SHIFTS = (1, 3, 2)
VMEM = pl.BlockSpec(memory_space=pltpu.VMEM)
SMEM = pl.BlockSpec(memory_space=pltpu.SMEM)
ANY = pl.BlockSpec(memory_space=pl.ANY)
PARAMS = pltpu.CompilerParams(vmem_limit_bytes=28 * 1024 * 1024)
LARGE = pltpu.CompilerParams(vmem_limit_bytes=60 * 1024 * 1024)


def split(a):
    hi = a.astype(BF16)
    return hi, (a - hi.astype(F32)).astype(BF16)


def dot(a, b, dims=((1,), (0,))):
    return lax.dot_general(a, b, (dims, ((), ())), preferred_element_type=F32)


def dot2(a, b, dims=((1,), (0,))):
    bh, bl = split(b)
    return dot(a, bh, dims) + dot(a, bl, dims)


def dot3(a, b, dims=((1,), (0,))):
    ah, al = split(a)
    bh, bl = split(b)
    return dot(ah, bh, dims) + (dot(ah, bl, dims) + dot(al, bh, dims))


def shape(dims, kind):
    return jax.ShapeDtypeStruct(dims, kind)


def from_next(a, axis, n, s):
    return lax.ppermute(a, axis, [(j, (j - s) % n) for j in range(n)])


def to_next(a, axis, n, s):
    return lax.ppermute(a, axis, [(j, (j + s) % n) for j in range(n)])


def exchange(wide, axis):
    return lax.all_to_all(wide, axis, split_axis=0, concat_axis=0)


def cost(flops, *arrays):
    moved = sum(a.size * a.dtype.itemsize for a in arrays)
    return pl.CostEstimate(flops=flops, bytes_accessed=moved, transcendentals=0)


def pack(tokens, out_grad, *factors):
    own, width = out_grad.shape
    own_features, rank = factors[0].shape
    ranks = rank * len(factors)
    groups = own_features // own

    def kernel(x, dy, *refs):
        out = refs[-1]
        out[:, :width] = x[...]
        out[:, width : 2 * width] = dy[...]
        halves = [split(ref[...]) for ref in refs[:-1]]
        order = [h[0] for h in halves[:-1]] + [h[1] for h in halves[:-1]] + list(halves[-1])
        for k in range(groups):
            for i, value in enumerate(order):
                at = 2 * width + k * 2 * ranks + i * rank
                out[:, at : at + rank] = value[k * own : (k + 1) * own]

    return pl.pallas_call(
        kernel,
        out_shape=shape((own, 2 * width + groups * 2 * ranks), BF16),
        in_specs=[VMEM] * (2 + len(factors)),
        out_specs=VMEM,
    )(tokens, out_grad, *factors)


def join_rows(here, cut, *parts):
    rows, lanes = parts[0].shape

    def kernel(here, *refs):
        left, right = refs[-2:]
        for s, ref in enumerate(refs[:-2]):
            at = pl.multiple_of(lax.rem(here[0] + s, len(parts)) * rows, rows)
            left[pl.ds(at, rows), :] = ref[:, :cut]
            right[pl.ds(at, rows), :] = ref[:, cut:]

    return pl.pallas_call(
        kernel,
        out_shape=(
            shape((rows * len(parts), cut), parts[0].dtype),
            shape((rows * len(parts), lanes - cut), parts[0].dtype),
        ),
        in_specs=[SMEM] + [VMEM] * len(parts),
        out_specs=(VMEM, VMEM),
    )(here, *parts)


def panel_moves(place, pieces, first, size, target, sems):
    y, c = place[1], place[2]
    moves = []
    for dc in range(NC):
        for d in range(NY):
            block = lax.rem(c + dc, NC) * NY + lax.rem(y + d, NY)
            piece = pieces[dc * NY + d]
            rows = piece.shape[0]
            moves.append(
                pltpu.make_async_copy(
                    piece.at[:, pl.ds(first, size)],
                    target.at[pl.ds(pl.multiple_of(block * rows, rows), rows)],
                    sems.at[dc * NY + d],
                )
            )
    return moves


def scaled(part, at, size, values, index, exponents):
    rows = part.shape[0]
    step = rows // 4
    top = jnp.float32(TINY)
    for k in range(0, rows, step):
        value = values(slice(k, k + step))
        part[k : k + step, at : at + size] = value
        top = jnp.maximum(top, jnp.max(jnp.abs(value)))
    exponent = jnp.ceil(jnp.log2(jnp.full((1, 128), top, F32))) - 15.0
    scale = jnp.exp2(-exponent)[:, :1]
    for k in range(0, rows, step):
        part[k : k + step, at : at + size] = part[k : k + step, at : at + size] * scale
    lane = lax.broadcasted_iota(jnp.int32, (1, 128), 1)
    return jnp.where(lane // 16 == index, exponent, exponents)


def forward_x(place, pieces, gate_w, up_w):
    quarter = pieces[0].shape[0]
    width, units = gate_w.shape
    rows = quarter * NY * NC

    def kernel(place, *refs):
        piece = refs[:8]
        gate, up, part, x, exponents_out, sem = refs[8:]
        moves = panel_moves(place, piece, 0, width, x, sem)
        for move in moves:
            move.start()
        for move in moves:
            move.wait()
        exponents = jnp.zeros((1, 128), F32)
        exponents = scaled(part, 0, units, lambda at: dot(x[at, :], gate[...]), 0, exponents)
        exponents = scaled(part, units, units, lambda at: dot(x[at, :], up[...]), 1, exponents)
        exponents_out[...] = jnp.broadcast_to(exponents, (8, 128))

    return pl.pallas_call(
        kernel,
        out_shape=(
            shape((rows, 2 * units), F32),
            shape((rows, width), BF16),
            shape((8, 128), F32),
        ),
        in_specs=[SMEM] + [VMEM] * 10,
        out_specs=(VMEM, VMEM, VMEM),
        scratch_shapes=[pltpu.SemaphoreType.DMA((8,))],
        compiler_params=PARAMS,
        cost_estimate=cost(33 * rows * width * units, gate_w, up_w),
    )(place, *pieces, gate_w, up_w)


def forward_dy(place, pieces, x, down_w, exponents, ranks, own_features):
    quarter, lanes = pieces[0].shape
    own = quarter // NZH
    rows, width = x.shape
    units = down_w.shape[0]
    rank = ranks // 3
    groups = own_features // own

    def kernel(place, *refs):
        piece = refs[:8]
        x, down, exponents_in, part, dy, factors, packed, sem_dy, sem_a = refs[8:]
        move_dy = panel_moves(place, piece, 0, width, dy, sem_dy)
        move_a = panel_moves(place, piece, width, lanes - width, packed, sem_a)
        for move in move_dy + move_a:
            move.start()
        for move in move_dy:
            move.wait()
        exponents = exponents_in[0:1, :]
        exponents = scaled(
            part, 0, units, lambda at: dot(dy[at, :], down[...], ((1,), (1,))), 2, exponents
        )
        for move in move_a:
            move.wait()
        for c in range(NC):
            for y in range(NY):
                for zh in range(NZH):
                    to = ((zh * NY + y) * NC + c) * own_features
                    at = ((c * NY + y) * NZH + zh) * own
                    for k in range(groups):
                        factors[to + k * own : to + (k + 1) * own, :] = packed[
                            at : at + own, k * 2 * ranks : (k + 1) * 2 * ranks
                        ]
        xa = dot(x[...], factors[:, : 2 * rank]) + dot(x[...], factors[:, 2 * rank : 4 * rank])
        dya = dot(dy[...], factors[:, 4 * rank :])
        dya = dya[:, :rank] + dya[:, rank:]
        values = (xa[:, :rank], xa[:, rank:], dya)
        for i, value in enumerate(values):
            exponents = scaled(
                part, units + i * rank, rank, lambda at: value[at, :], 3 + i, exponents
            )
        part[:, units + ranks :] = jnp.broadcast_to(exponents, (rows, 128))

    return pl.pallas_call(
        kernel,
        out_shape=(
            shape((rows, units + ranks + 128), F32),
            shape((rows, width), BF16),
            shape((width, 2 * ranks), BF16),
        ),
        in_specs=[SMEM] + [VMEM] * 11,
        out_specs=(VMEM, VMEM, VMEM),
        scratch_shapes=[
            pltpu.VMEM((rows, lanes - width), BF16),
            pltpu.SemaphoreType.DMA((8,)),
            pltpu.SemaphoreType.DMA((8,)),
        ],
        compiler_params=PARAMS,
        cost_estimate=cost(38 * rows * width * units, down_w, x),
    )(place, *pieces, x, down_w, exponents)


def swiglu_back(first, second, b_parts):
    per, lanes = second.shape[1:]
    share, units = b_parts.shape[1] // 3, b_parts.shape[2]
    rank = share * NROW
    ranks = 3 * rank
    sizes = [units] * 3 + [rank] * 3
    starts = [0, units, 0, units, units + rank, units + 2 * rank]

    def kernel(first, second, b_parts, wide, g_out, factor_out, b):
        for i in range(3):
            for r in range(NROW):
                b[i, r * share : (r + 1) * share, :] = b_parts[r, i * share : (i + 1) * share, :]
        scales = [jnp.exp2(second[r, 0:1, lanes - 128 :]) for r in range(NROW)]

        def total(i):
            value = 0.0
            sums = first if i < 2 else second
            for r in range(NROW):
                part = sums[r, :, starts[i] : starts[i] + sizes[i]]
                value = value + part * scales[r][:, 16 * i : 16 * i + 1]
            return value

        products = [total(3 + i) for i in range(3)]
        gate_pre, up_pre, grad_hidden = (total(i) + dot3(products[i], b[i]) for i in range(3))
        sigma = 1.0 / (1.0 + jnp.exp(-gate_pre))
        hidden = (gate_pre * sigma * up_pre).astype(BF16)
        d_gate = (grad_hidden * up_pre * sigma * (1.0 + gate_pre * (1.0 - sigma))).astype(BF16)
        d_up = (grad_hidden * gate_pre * sigma).astype(BF16)
        for r in range(NROW):
            wide[r, :, :units] = d_gate
            wide[r, :, units:] = d_up
        for i, d in enumerate((d_gate, d_up, hidden)):
            g_out[:, i * rank : (i + 1) * rank] = dot2(d, b[i], ((1,), (1,)))
            hi, lo = split(products[i].T)
            grad = dot(hi, d) + dot(lo, d)
            for r in range(NROW):
                factor_out[r, i * share : (i + 1) * share, :] = grad[
                    r * share : (r + 1) * share
                ].astype(BF16)

    return pl.pallas_call(
        kernel,
        out_shape=(
            shape((NROW, per, 2 * units), BF16),
            shape((per, ranks), F32),
            shape((NROW, 3 * share, units), BF16),
        ),
        in_specs=[VMEM] * 3,
        out_specs=(VMEM,) * 3,
        scratch_shapes=[pltpu.VMEM((3, rank, units), F32)],
        compiler_params=PARAMS,
        cost_estimate=cost(24 * per * rank * units, first, second),
    )(first, second, b_parts)


def backward(which, d_all, gate_w, up_w):
    half = d_all.shape[0] // NC
    width, units = gate_w.shape

    def kernel(which, d, gate, up, out):
        at = pl.ds(pl.multiple_of(which[0] * half, half), half)
        out[...] = dot(d[at, :units], gate[...], ((1,), (1,))) + dot(
            d[at, units:], up[...], ((1,), (1,))
        )

    return pl.pallas_call(
        kernel,
        out_shape=shape((half, width), F32),
        in_specs=[SMEM] + [VMEM] * 3,
        out_specs=VMEM,
        compiler_params=PARAMS,
        cost_estimate=cost(4 * half * width * units, gate_w, up_w),
    )(which, d_all, gate_w, up_w)


def add_and_cut(here, kind, *parts):
    rows, width = parts[0].shape
    block = rows // 4

    def kernel(here, *refs):
        ins, outs = refs[: len(parts)], refs[len(parts) :]
        for s, out in zip((0,) + SHIFTS, outs):
            at = pl.ds(pl.multiple_of(lax.rem(here[0] + s, 4) * block, block), block)
            total = ins[0][at, :].astype(F32)
            for ref in ins[1:]:
                total = total + ref[at, :].astype(F32)
            out[...] = total.astype(out.dtype)

    return pl.pallas_call(
        kernel,
        out_shape=(shape((block, width), F32),) + (shape((block, width), kind),) * 3,
        in_specs=[SMEM] + [VMEM] * len(parts),
        out_specs=(VMEM,) * 4,
        compiler_params=PARAMS,
    )(here, *parts)


def merge(factor_parts, g):
    share, units = factor_parts.shape[1:]
    per, ranks = g.shape

    def kernel(parts, g, out):
        hi, lo = split(g[...])
        for r in range(NROW):
            out[r, :share, :] = parts[r]
            out[r, share:, :ranks] = hi
            out[r, share:, ranks : 2 * ranks] = lo
            out[r, share:, 2 * ranks :] = jnp.zeros((per, units - 2 * ranks), BF16)

    return pl.pallas_call(
        kernel,
        out_shape=shape((NROW, share + per, units), BF16),
        in_specs=[VMEM] * 2,
        out_specs=VMEM,
    )(factor_parts, g)


def select(place, x, dy, own_features):
    rows, width = x.shape

    def kernel(place, x, dy, out):
        y, c = place[1], place[2]
        row = lax.broadcasted_iota(jnp.int32, (own_features, width), 0)
        lane = lax.broadcasted_iota(jnp.int32, (own_features, width), 1)
        for zh in range(NZH):
            start = ((zh * NY + y) * NC + c) * own_features
            pick = jnp.where(lane == row + start, 1.0, 0.0).astype(BF16)
            for i, panel in enumerate((x, dy)):
                at = (i * NZH + zh) * own_features
                out[at : at + own_features, :] = dot(pick, panel[...], ((1,), (1,))).astype(BF16)

    return pl.pallas_call(
        kernel,
        out_shape=shape((2 * NZH * own_features, rows), BF16),
        in_specs=[SMEM, VMEM, VMEM],
        out_specs=VMEM,
        compiler_params=PARAMS,
        cost_estimate=cost(4 * NZH * own_features * rows * width, x, dy),
    )(place, x, dy)


def rank_grads(place, selected, merged, factors, ranks):
    features = selected.shape[0] // 2
    rows = selected.shape[1]
    per = rows // NROW
    rank = ranks // 3
    share = merged.shape[1] - per
    width = factors.shape[0]

    def kernel(place, selected, merged, factors, grads, adapter, g):
        for r in range(NROW):
            g[r * per : (r + 1) * per, :] = merged[r, share:, : 2 * ranks]
        hi, lo = g[:, :ranks], g[:, ranks:]
        xs, dys = selected[:features, :], selected[features:, :]
        grads[:, : 2 * rank] = dot(xs, hi[:, : 2 * rank]) + dot(xs, lo[:, : 2 * rank])
        grads[:, 2 * rank :] = dot(dys, hi[:, 2 * rank :]) + dot(dys, lo[:, 2 * rank :])
        block = place[2] * NY + place[1]
        own = g[pl.ds(pl.multiple_of(block * per, per), per), :]
        gh, gl = own[:, : 2 * rank], own[:, ranks : ranks + 2 * rank]
        ah, al = factors[:, : 2 * rank], factors[:, 2 * rank : 4 * rank]
        last = ((1,), (1,))
        adapter[...] = dot(gh, ah, last) + (dot(gl, ah, last) + dot(gh, al, last))

    return pl.pallas_call(
        kernel,
        out_shape=(shape((features, ranks), F32), shape((per, width), F32)),
        in_specs=[SMEM] + [VMEM] * 3,
        out_specs=(VMEM, VMEM),
        scratch_shapes=[pltpu.VMEM((rows, 2 * ranks), BF16)],
        compiler_params=PARAMS,
    )(place, selected, merged, factors)


def cut_last(here, grads, *parts):
    rows, width = parts[0].shape
    block = rows // NZH
    features = grads.shape[0] // NZH
    ranks = grads.shape[1]
    groups = features // block
    lanes = width + groups * ranks

    def kernel(here, grads, *refs):
        ins, (own, wide) = refs[: len(parts)], refs[len(parts) :]

        def fill(to, out):
            at = pl.ds(pl.multiple_of(to * block, block), block)
            total = ins[0][at, :].astype(F32)
            for ref in ins[1:]:
                total = total + ref[at, :].astype(F32)
            out[:, :width] = total.astype(out.dtype)
            for k in range(groups):
                at = pl.ds(pl.multiple_of(to * features + k * block, block), block)
                out[:, width + k * ranks : width + (k + 1) * ranks] = grads[at, :].astype(out.dtype)

        fill(here[0], own)
        for zh in range(NZH):
            fill(zh, wide.at[zh])
        wide[here[0]] = jnp.zeros((block, lanes), wide.dtype)

    return pl.pallas_call(
        kernel,
        out_shape=(shape((block, lanes), F32), shape((NZH, block, lanes), BF16)),
        in_specs=[SMEM] + [VMEM] * (1 + len(parts)),
        out_specs=(VMEM,) * 2,
        compiler_params=PARAMS,
    )(here, grads, *parts)


def finish(width, rank, kept, others):
    own, lanes = kept.shape
    ranks = 3 * rank
    groups = (lanes - width) // ranks

    def kernel(kept, others, tokens, *factors):
        total = kept[...]
        for zh in range(NZH):
            total = total + others[zh].astype(F32)
        tokens[...] = total[:, :width]
        for k in range(groups):
            for i, out in enumerate(factors):
                at = width + k * ranks + i * rank
                out[k * own : (k + 1) * own, :] = total[:, at : at + rank]

    return pl.pallas_call(
        kernel,
        out_shape=(shape((own, width), F32),) + (shape((own * groups, rank), F32),) * 3,
        in_specs=[VMEM] * 2,
        out_specs=(VMEM,) * 4,
    )(kept, others)


def after(value, *others):
    return lax.optimization_barrier((value,) + others)[0]


def body(tokens, out_grad, gate_w, up_w, down_w, gate_a, up_a, down_b_t, gate_b, up_b, down_a_t):
    own, width = tokens.shape
    units = gate_w.shape[1]
    own_features, rank = gate_a.shape
    zh, y, c = (lax.axis_index(a) for a in COL)
    row = lax.axis_index(ROW)
    place = jnp.stack([zh, y, c, row]).astype(jnp.int32)

    at_zh, at_y, at_c, at_other = (
        v.reshape(1).astype(jnp.int32) for v in (zh, y, c, (c + 1) % NC)
    )
    ranks = 3 * rank

    mine = pack(tokens, out_grad, gate_a, up_a, down_b_t)
    got = {0: mine}
    for s in SHIFTS:
        got[s] = from_next(mine, "zh", NZH, s)
    near, late = join_rows(at_zh, width, *[got[s] for s in range(NZH)])

    def from_y(a):
        got = {0: a}
        for s in SHIFTS:
            got[s] = from_next(a, "y", NY, s)
        return [got[s] for s in range(NY)]

    def with_core(pieces):
        return pieces + [from_next(p, "c", NC, 1) for p in pieces]

    pieces = from_y(near)
    late_pieces = from_y(after(late, *pieces[1:]))
    b_own = after(jnp.concatenate([gate_b, up_b, down_a_t], axis=0), near)
    b_parts = exchange(jnp.broadcast_to(b_own[None], (NROW,) + b_own.shape), ROW)
    pieces = with_core(pieces)

    def half(part):
        return part.astype(F16).reshape(NROW, rows // NROW, part.shape[1])

    part_x, x, exponents = forward_x(place, pieces, gate_w, up_w)
    rows = x.shape[0]
    part_x, b_parts = lax.optimization_barrier((half(part_x), b_parts))
    *late_pieces, exponents = lax.optimization_barrier((*late_pieces, exponents))
    part_dy, dy, factors = forward_dy(
        place, with_core(late_pieces), x, down_w, exponents, ranks, own_features
    )
    sums_x, part_dy = lax.optimization_barrier((exchange(part_x, ROW), half(part_dy)))
    selected = select(place, x, dy, own_features)
    wide, g, factor_parts = swiglu_back(
        sums_x.astype(F32), exchange(part_dy, ROW).astype(F32), b_parts
    )

    d_all = exchange(wide, ROW).reshape(rows, 2 * units)

    g = g + from_next(g, "c", NC, 1)
    g = g + sum(from_next(g, "y", NY, s) for s in SHIFTS)
    merged = merge(factor_parts, g)
    d_all, merged, selected = lax.optimization_barrier((d_all, merged, selected))
    merged = exchange(merged, ROW)

    sent = backward(at_other, d_all, gate_w, up_w)
    other = from_next(sent, "c", NC, 1)
    kept = backward(at_c, after(d_all, sent), gate_w, up_w)
    kept, *sends = add_and_cut(at_y, BF16, kept, other)
    others = [to_next(a, "y", NY, s) for s, a in zip(SHIFTS, sends)]

    grads, adapter = rank_grads(place, selected, merged, factors, ranks)
    kept, sends = cut_last(at_zh, grads, kept, *others, adapter)
    grad_tokens, grad_gate_a, grad_up_a, grad_down_b_t = finish(
        width, rank, kept, exchange(sends, "zh")
    )

    share = gate_b.shape[0]
    factor_grads = merged[:, : 3 * share].astype(F32).sum(0)
    grad_b = [factor_grads[i * share : (i + 1) * share] for i in range(3)]
    return (grad_tokens, grad_gate_a, grad_up_a, *grad_b, grad_down_b_t)


def solution(mesh):
    fine = Mesh(mesh.devices.reshape(NX, NZL, NZH, NY, NC), ROW + COL)
    tiled = P(COL, ROW)
    weight = P(ROW, COL)
    factor = P(ROW + COL, None)
    return jax.shard_map(
        body,
        mesh=fine,
        in_specs=(tiled, tiled, weight, weight, tiled, factor, factor, factor, weight, weight, weight),
        out_specs=(tiled, factor, factor, weight, weight, weight, factor),
        check_vma=False,
    )
```

```python
import jax
import jax.numpy as jnp
from jax import lax
from jax.experimental import pallas as pl
from jax.experimental.pallas import tpu as pltpu
from jax.sharding import Mesh, PartitionSpec as P

ROW = ("x", "zl")
COL = ("zh", "y", "c")
NX, NZL, NZH, NY, NC = 4, 2, 4, 4, 2
NROW = NX * NZL
F32, F16, BF16 = jnp.float32, jnp.float16, jnp.bfloat16
F16_TOP = 32768.0
TINY = 1e-30
SHIFTS = (1, 3, 2)
VMEM = pl.BlockSpec(memory_space=pltpu.VMEM)
SMEM = pl.BlockSpec(memory_space=pltpu.SMEM)
ANY = pl.BlockSpec(memory_space=pl.ANY)
PARAMS = pltpu.CompilerParams(vmem_limit_bytes=28 * 1024 * 1024)
LARGE = pltpu.CompilerParams(vmem_limit_bytes=60 * 1024 * 1024)


def split(a):
    hi = a.astype(BF16)
    return hi, (a - hi.astype(F32)).astype(BF16)


def dot(a, b, dims=((1,), (0,))):
    return lax.dot_general(a, b, (dims, ((), ())), preferred_element_type=F32)


def dot2(a, b, dims=((1,), (0,))):
    bh, bl = split(b)
    return dot(a, bh, dims) + dot(a, bl, dims)


def dot3(a, b, dims=((1,), (0,))):
    ah, al = split(a)
    bh, bl = split(b)
    return dot(ah, bh, dims) + (dot(ah, bl, dims) + dot(al, bh, dims))


def shape(dims, kind):
    return jax.ShapeDtypeStruct(dims, kind)


def from_next(a, axis, n, s):
    return lax.ppermute(a, axis, [(j, (j - s) % n) for j in range(n)])


def to_next(a, axis, n, s):
    return lax.ppermute(a, axis, [(j, (j + s) % n) for j in range(n)])


def exchange(wide, axis):
    return lax.all_to_all(wide, axis, split_axis=0, concat_axis=0)


def cost(flops, *arrays):
    moved = sum(a.size * a.dtype.itemsize for a in arrays)
    return pl.CostEstimate(flops=flops, bytes_accessed=moved, transcendentals=0)


def pack(tokens, out_grad, *factors):
    own, width = out_grad.shape
    own_features, rank = factors[0].shape
    ranks = rank * len(factors)
    groups = own_features // own

    def kernel(x, dy, *refs):
        out = refs[-1]
        out[:, :width] = x[...]
        out[:, width : 2 * width] = dy[...]
        halves = [split(ref[...]) for ref in refs[:-1]]
        order = [h[0] for h in halves[:-1]] + [h[1] for h in halves[:-1]] + list(halves[-1])
        for k in range(groups):
            for i, value in enumerate(order):
                at = 2 * width + k * 2 * ranks + i * rank
                out[:, at : at + rank] = value[k * own : (k + 1) * own]

    return pl.pallas_call(
        kernel,
        out_shape=shape((own, 2 * width + groups * 2 * ranks), BF16),
        in_specs=[VMEM] * (2 + len(factors)),
        out_specs=VMEM,
    )(tokens, out_grad, *factors)


def join_rows(here, cut, *parts):
    rows, lanes = parts[0].shape

    def kernel(here, *refs):
        left, right = refs[-2:]
        for s, ref in enumerate(refs[:-2]):
            at = pl.multiple_of(lax.rem(here[0] + s, len(parts)) * rows, rows)
            left[pl.ds(at, rows), :] = ref[:, :cut]
            right[pl.ds(at, rows), :] = ref[:, cut:]

    return pl.pallas_call(
        kernel,
        out_shape=(
            shape((rows * len(parts), cut), parts[0].dtype),
            shape((rows * len(parts), lanes - cut), parts[0].dtype),
        ),
        in_specs=[SMEM] + [VMEM] * len(parts),
        out_specs=(VMEM, VMEM),
    )(here, *parts)


def order_factors(b_parts):
    share, units = b_parts.shape[1] // 3, b_parts.shape[2]

    def kernel(b_parts, b):
        for i in range(3):
            for r in range(NROW):
                b[i, r * share : (r + 1) * share, :] = b_parts[r, i * share : (i + 1) * share, :]

    return pl.pallas_call(
        kernel,
        out_shape=shape((3, NROW * share, units), F32),
        in_specs=[VMEM],
        out_specs=VMEM,
        compiler_params=PARAMS,
        cost_estimate=cost(0, b_parts, b_parts),
    )(b_parts)


def panel_moves(place, pieces, first, size, target, sems):
    y, c = place[1], place[2]
    moves = []
    for dc in range(NC):
        for d in range(NY):
            block = lax.rem(c + dc, NC) * NY + lax.rem(y + d, NY)
            piece = pieces[dc * NY + d]
            rows = piece.shape[0]
            moves.append(
                pltpu.make_async_copy(
                    piece.at[:, pl.ds(first, size)],
                    target.at[pl.ds(pl.multiple_of(block * rows, rows), rows)],
                    sems.at[dc * NY + d],
                )
            )
    return moves


def scaled(part, at, size, values, index, exponents):
    rows = part.shape[0]
    step = rows // 4
    top = jnp.float32(TINY)
    for k in range(0, rows, step):
        value = values(slice(k, k + step))
        part[k : k + step, at : at + size] = value
        top = jnp.maximum(top, jnp.max(jnp.abs(value)))
    exponent = jnp.ceil(jnp.log2(jnp.full((1, 128), top, F32))) - 15.0
    scale = jnp.exp2(-exponent)[:, :1]
    for k in range(0, rows, step):
        part[k : k + step, at : at + size] = part[k : k + step, at : at + size] * scale
    lane = lax.broadcasted_iota(jnp.int32, (1, 128), 1)
    return jnp.where(lane // 16 == index, exponent, exponents)


def forward_x(place, pieces, gate_w, up_w):
    quarter = pieces[0].shape[0]
    width, units = gate_w.shape
    rows = quarter * NY * NC

    def kernel(place, *refs):
        piece = refs[:8]
        gate, up, part, x, exponents_out, sem = refs[8:]
        moves = panel_moves(place, piece, 0, width, x, sem)
        for move in moves:
            move.start()
        for move in moves:
            move.wait()
        exponents = jnp.zeros((1, 128), F32)
        exponents = scaled(part, 0, units, lambda at: dot(x[at, :], gate[...]), 0, exponents)
        exponents = scaled(part, units, units, lambda at: dot(x[at, :], up[...]), 1, exponents)
        exponents_out[...] = jnp.broadcast_to(exponents, (8, 128))

    return pl.pallas_call(
        kernel,
        out_shape=(
            shape((rows, 2 * units), F32),
            shape((rows, width), BF16),
            shape((8, 128), F32),
        ),
        in_specs=[SMEM] + [VMEM] * 10,
        out_specs=(VMEM, VMEM, VMEM),
        scratch_shapes=[pltpu.SemaphoreType.DMA((8,))],
        compiler_params=PARAMS,
        cost_estimate=cost(33 * rows * width * units, gate_w, up_w),
    )(place, *pieces, gate_w, up_w)


def forward_dy(place, pieces, x, down_w, exponents, ranks, own_features):
    quarter, lanes = pieces[0].shape
    own = quarter // NZH
    rows, width = x.shape
    units = down_w.shape[0]
    rank = ranks // 3
    groups = own_features // own

    def kernel(place, *refs):
        piece = refs[:8]
        x, down, exponents_in, part, dy, factors, packed, sem_dy, sem_a = refs[8:]
        move_dy = panel_moves(place, piece, 0, width, dy, sem_dy)
        move_a = panel_moves(place, piece, width, lanes - width, packed, sem_a)
        for move in move_dy + move_a:
            move.start()
        for move in move_dy:
            move.wait()
        exponents = exponents_in[0:1, :]
        exponents = scaled(
            part, 0, units, lambda at: dot(dy[at, :], down[...], ((1,), (1,))), 2, exponents
        )
        for move in move_a:
            move.wait()
        for c in range(NC):
            for y in range(NY):
                for zh in range(NZH):
                    to = ((zh * NY + y) * NC + c) * own_features
                    at = ((c * NY + y) * NZH + zh) * own
                    for k in range(groups):
                        factors[to + k * own : to + (k + 1) * own, :] = packed[
                            at : at + own, k * 2 * ranks : (k + 1) * 2 * ranks
                        ]
        xa = dot(x[...], factors[:, : 2 * rank]) + dot(x[...], factors[:, 2 * rank : 4 * rank])
        dya = dot(dy[...], factors[:, 4 * rank :])
        dya = dya[:, :rank] + dya[:, rank:]
        values = (xa[:, :rank], xa[:, rank:], dya)
        for i, value in enumerate(values):
            exponents = scaled(
                part, units + i * rank, rank, lambda at: value[at, :], 3 + i, exponents
            )
        part[:, units + ranks :] = jnp.broadcast_to(exponents, (rows, 128))

    return pl.pallas_call(
        kernel,
        out_shape=(
            shape((rows, units + ranks + 128), F32),
            shape((rows, width), BF16),
            shape((width, 2 * ranks), BF16),
        ),
        in_specs=[SMEM] + [VMEM] * 11,
        out_specs=(VMEM, VMEM, VMEM),
        scratch_shapes=[
            pltpu.VMEM((rows, lanes - width), BF16),
            pltpu.SemaphoreType.DMA((8,)),
            pltpu.SemaphoreType.DMA((8,)),
        ],
        compiler_params=PARAMS,
        cost_estimate=cost(38 * rows * width * units, down_w, x),
    )(place, *pieces, x, down_w, exponents)


def swiglu_back(first, second, b):
    per, lanes = second.shape[1:]
    rank, units = b.shape[1:]
    share = rank // NROW
    ranks = 3 * rank
    sizes = [units] * 3 + [rank] * 3
    starts = [0, units, 0, units, units + rank, units + 2 * rank]

    def kernel(first, second, b, wide, g_out, factor_out):
        scales = [jnp.exp2(second[r, 0:1, lanes - 128 :]) for r in range(NROW)]

        def total(i):
            value = 0.0
            sums = first if i < 2 else second
            for r in range(NROW):
                part = sums[r, :, starts[i] : starts[i] + sizes[i]]
                value = value + part * scales[r][:, 16 * i : 16 * i + 1]
            return value

        products = [total(3 + i) for i in range(3)]
        gate_pre, up_pre, grad_hidden = (total(i) + dot3(products[i], b[i]) for i in range(3))
        sigma = 1.0 / (1.0 + jnp.exp(-gate_pre))
        hidden = (gate_pre * sigma * up_pre).astype(BF16)
        d_gate = (grad_hidden * up_pre * sigma * (1.0 + gate_pre * (1.0 - sigma))).astype(BF16)
        d_up = (grad_hidden * gate_pre * sigma).astype(BF16)
        for r in range(NROW):
            wide[r, :, :units] = d_gate
            wide[r, :, units:] = d_up
        for i, d in enumerate((d_gate, d_up, hidden)):
            g_out[:, i * rank : (i + 1) * rank] = dot2(d, b[i], ((1,), (1,)))
            hi, lo = split(products[i].T)
            grad = dot(hi, d) + dot(lo, d)
            for r in range(NROW):
                factor_out[r, i * share : (i + 1) * share, :] = grad[
                    r * share : (r + 1) * share
                ].astype(BF16)

    return pl.pallas_call(
        kernel,
        out_shape=(
            shape((NROW, per, 2 * units), BF16),
            shape((per, ranks), F32),
            shape((NROW, 3 * share, units), BF16),
        ),
        in_specs=[VMEM] * 3,
        out_specs=(VMEM,) * 3,
        compiler_params=PARAMS,
        cost_estimate=cost(24 * per * rank * units, first, second),
    )(first, second, b)


def backward(which, d_all, gate_w, up_w):
    half = d_all.shape[0] // NC
    width, units = gate_w.shape

    def kernel(which, d, gate, up, out):
        at = pl.ds(pl.multiple_of(which[0] * half, half), half)
        out[...] = dot(d[at, :units], gate[...], ((1,), (1,))) + dot(
            d[at, units:], up[...], ((1,), (1,))
        )

    return pl.pallas_call(
        kernel,
        out_shape=shape((half, width), F32),
        in_specs=[SMEM] + [VMEM] * 3,
        out_specs=VMEM,
        compiler_params=PARAMS,
        cost_estimate=cost(4 * half * width * units, gate_w, up_w),
    )(which, d_all, gate_w, up_w)


def add_and_cut(here, kind, *parts):
    rows, width = parts[0].shape
    block = rows // 4

    def kernel(here, *refs):
        ins, outs = refs[: len(parts)], refs[len(parts) :]
        for s, out in zip((0,) + SHIFTS, outs):
            at = pl.ds(pl.multiple_of(lax.rem(here[0] + s, 4) * block, block), block)
            total = ins[0][at, :].astype(F32)
            for ref in ins[1:]:
                total = total + ref[at, :].astype(F32)
            out[...] = total.astype(out.dtype)

    return pl.pallas_call(
        kernel,
        out_shape=(shape((block, width), F32),) + (shape((block, width), kind),) * 3,
        in_specs=[SMEM] + [VMEM] * len(parts),
        out_specs=(VMEM,) * 4,
        compiler_params=PARAMS,
    )(here, *parts)


def merge(factor_parts, g):
    share, units = factor_parts.shape[1:]
    per, ranks = g.shape

    def kernel(parts, g, out):
        hi, lo = split(g[...])
        for r in range(NROW):
            out[r, :share, :] = parts[r]
            out[r, share:, :ranks] = hi
            out[r, share:, ranks : 2 * ranks] = lo
            out[r, share:, 2 * ranks :] = jnp.zeros((per, units - 2 * ranks), BF16)

    return pl.pallas_call(
        kernel,
        out_shape=shape((NROW, share + per, units), BF16),
        in_specs=[VMEM] * 2,
        out_specs=VMEM,
    )(factor_parts, g)


def select(place, x, dy, own_features):
    rows, width = x.shape

    def kernel(place, x, dy, out):
        y, c = place[1], place[2]
        row = lax.broadcasted_iota(jnp.int32, (own_features, width), 0)
        lane = lax.broadcasted_iota(jnp.int32, (own_features, width), 1)
        for zh in range(NZH):
            start = ((zh * NY + y) * NC + c) * own_features
            pick = jnp.where(lane == row + start, 1.0, 0.0).astype(BF16)
            for i, panel in enumerate((x, dy)):
                at = (i * NZH + zh) * own_features
                out[at : at + own_features, :] = dot(pick, panel[...], ((1,), (1,))).astype(BF16)

    return pl.pallas_call(
        kernel,
        out_shape=shape((2 * NZH * own_features, rows), BF16),
        in_specs=[SMEM, VMEM, VMEM],
        out_specs=VMEM,
        compiler_params=PARAMS,
        cost_estimate=cost(4 * NZH * own_features * rows * width, x, dy),
    )(place, x, dy)


def rank_grads(place, selected, merged, factors, ranks):
    features = selected.shape[0] // 2
    rows = selected.shape[1]
    per = rows // NROW
    rank = ranks // 3
    share = merged.shape[1] - per
    width = factors.shape[0]

    def kernel(place, selected, merged, factors, grads, adapter, g):
        for r in range(NROW):
            g[r * per : (r + 1) * per, :] = merged[r, share:, : 2 * ranks]
        hi, lo = g[:, :ranks], g[:, ranks:]
        xs, dys = selected[:features, :], selected[features:, :]
        grads[:, : 2 * rank] = dot(xs, hi[:, : 2 * rank]) + dot(xs, lo[:, : 2 * rank])
        grads[:, 2 * rank :] = dot(dys, hi[:, 2 * rank :]) + dot(dys, lo[:, 2 * rank :])
        block = place[2] * NY + place[1]
        own = g[pl.ds(pl.multiple_of(block * per, per), per), :]
        gh, gl = own[:, : 2 * rank], own[:, ranks : ranks + 2 * rank]
        ah, al = factors[:, : 2 * rank], factors[:, 2 * rank : 4 * rank]
        last = ((1,), (1,))
        adapter[...] = dot(gh, ah, last) + (dot(gl, ah, last) + dot(gh, al, last))

    return pl.pallas_call(
        kernel,
        out_shape=(shape((features, ranks), F32), shape((per, width), F32)),
        in_specs=[SMEM] + [VMEM] * 3,
        out_specs=(VMEM, VMEM),
        scratch_shapes=[pltpu.VMEM((rows, 2 * ranks), BF16)],
        compiler_params=PARAMS,
    )(place, selected, merged, factors)


def cut_last(here, grads, *parts):
    rows, width = parts[0].shape
    block = rows // NZH
    features = grads.shape[0] // NZH
    ranks = grads.shape[1]
    groups = features // block
    lanes = width + groups * ranks

    def kernel(here, grads, *refs):
        ins, (own, wide) = refs[: len(parts)], refs[len(parts) :]

        def fill(to, out):
            at = pl.ds(pl.multiple_of(to * block, block), block)
            total = ins[0][at, :].astype(F32)
            for ref in ins[1:]:
                total = total + ref[at, :].astype(F32)
            out[:, :width] = total.astype(out.dtype)
            for k in range(groups):
                at = pl.ds(pl.multiple_of(to * features + k * block, block), block)
                out[:, width + k * ranks : width + (k + 1) * ranks] = grads[at, :].astype(out.dtype)

        fill(here[0], own)
        for zh in range(NZH):
            fill(zh, wide.at[zh])
        wide[here[0]] = jnp.zeros((block, lanes), wide.dtype)

    return pl.pallas_call(
        kernel,
        out_shape=(shape((block, lanes), F32), shape((NZH, block, lanes), BF16)),
        in_specs=[SMEM] + [VMEM] * (1 + len(parts)),
        out_specs=(VMEM,) * 2,
        compiler_params=PARAMS,
    )(here, grads, *parts)


def finish(width, rank, kept, others):
    own, lanes = kept.shape
    ranks = 3 * rank
    groups = (lanes - width) // ranks

    def kernel(kept, others, tokens, *factors):
        total = kept[...]
        for zh in range(NZH):
            total = total + others[zh].astype(F32)
        tokens[...] = total[:, :width]
        for k in range(groups):
            for i, out in enumerate(factors):
                at = width + k * ranks + i * rank
                out[k * own : (k + 1) * own, :] = total[:, at : at + rank]

    return pl.pallas_call(
        kernel,
        out_shape=(shape((own, width), F32),) + (shape((own * groups, rank), F32),) * 3,
        in_specs=[VMEM] * 2,
        out_specs=(VMEM,) * 4,
    )(kept, others)


def after(value, *others):
    return lax.optimization_barrier((value,) + others)[0]


def body(tokens, out_grad, gate_w, up_w, down_w, gate_a, up_a, down_b_t, gate_b, up_b, down_a_t):
    own, width = tokens.shape
    units = gate_w.shape[1]
    own_features, rank = gate_a.shape
    zh, y, c = (lax.axis_index(a) for a in COL)
    row = lax.axis_index(ROW)
    place = jnp.stack([zh, y, c, row]).astype(jnp.int32)

    at_zh, at_y, at_c, at_other = (
        v.reshape(1).astype(jnp.int32) for v in (zh, y, c, (c + 1) % NC)
    )
    ranks = 3 * rank

    mine = pack(tokens, out_grad, gate_a, up_a, down_b_t)
    got = {0: mine}
    for s in SHIFTS:
        got[s] = from_next(mine, "zh", NZH, s)
    near, late = join_rows(at_zh, width, *[got[s] for s in range(NZH)])

    def from_y(a):
        got = {0: a}
        for s in SHIFTS:
            got[s] = from_next(a, "y", NY, s)
        return [got[s] for s in range(NY)]

    def with_core(pieces):
        return pieces + [from_next(p, "c", NC, 1) for p in pieces]

    pieces = from_y(near)
    late_pieces = from_y(after(late, *pieces[1:]))
    b_own = after(jnp.concatenate([gate_b, up_b, down_a_t], axis=0), near)
    b_parts = exchange(jnp.broadcast_to(b_own[None], (NROW,) + b_own.shape), ROW)
    pieces = with_core(pieces)

    def half(part):
        return part.astype(F16).reshape(NROW, rows // NROW, part.shape[1])

    part_x, x, exponents = forward_x(place, pieces, gate_w, up_w)
    rows = x.shape[0]
    part_x, b_parts = lax.optimization_barrier((half(part_x), b_parts))
    *late_pieces, exponents = lax.optimization_barrier((*late_pieces, exponents))
    part_dy, dy, factors = forward_dy(
        place, with_core(late_pieces), x, down_w, exponents, ranks, own_features
    )
    sums_x, part_dy = lax.optimization_barrier((exchange(part_x, ROW), half(part_dy)))
    sums_dy, selected, b = lax.optimization_barrier(
        (exchange(part_dy, ROW), select(place, x, dy, own_features), order_factors(b_parts))
    )
    wide, g, factor_parts = swiglu_back(sums_x.astype(F32), sums_dy.astype(F32), b)

    d_all = exchange(wide, ROW).reshape(rows, 2 * units)

    g = g + from_next(g, "c", NC, 1)
    g = g + sum(from_next(g, "y", NY, s) for s in SHIFTS)
    merged = merge(factor_parts, g)
    d_all, merged, selected = lax.optimization_barrier((d_all, merged, selected))
    merged = exchange(merged, ROW)

    sent = backward(at_other, d_all, gate_w, up_w)
    other = from_next(sent, "c", NC, 1)
    kept = backward(at_c, after(d_all, sent), gate_w, up_w)
    kept, *sends = add_and_cut(at_y, BF16, kept, other)
    others = [to_next(a, "y", NY, s) for s, a in zip(SHIFTS, sends)]

    grads, adapter = rank_grads(place, selected, merged, factors, ranks)
    kept, sends = cut_last(at_zh, grads, kept, *others, adapter)
    grad_tokens, grad_gate_a, grad_up_a, grad_down_b_t = finish(
        width, rank, kept, exchange(sends, "zh")
    )

    share = gate_b.shape[0]
    factor_grads = merged[:, : 3 * share].astype(F32).sum(0)
    grad_b = [factor_grads[i * share : (i + 1) * share] for i in range(3)]
    return (grad_tokens, grad_gate_a, grad_up_a, *grad_b, grad_down_b_t)


def solution(mesh):
    fine = Mesh(mesh.devices.reshape(NX, NZL, NZH, NY, NC), ROW + COL)
    tiled = P(COL, ROW)
    weight = P(ROW, COL)
    factor = P(ROW + COL, None)
    return jax.shard_map(
        body,
        mesh=fine,
        in_specs=(tiled, tiled, weight, weight, tiled, factor, factor, factor, weight, weight, weight),
        out_specs=(tiled, factor, factor, weight, weight, weight, factor),
        check_vma=False,
    )
```
